128 devices in a mesh: enc: 4 (over y), pool: 32 (over z, x, core).
Axes of the slice: x: 4, y: 4, z: 4, core: 2. Of those that a mesh axis runs over, the one named last changes fastest.
Arguments:
- encoded: bfloat16 [8192, 32, 128], P('pool', 'enc'), may hold values from -6 to 6
- slot_items: int32 [8192], replicated, may hold values from 0 to 8191, as said below
- lengths: int32 [8192], P(('enc', 'pool')), may hold values from 1 to 32
- token_mask: int32 [8192, 32], P(('enc', 'pool')), may hold values 0 or 1
Outputs:
- scores: float32 [8192, 192], P(('enc', 'pool'))
The draws below stay inside these ranges and needn't reach their ends.
Inputs may be any that keep to these rules, and one draw needn't show every extreme that they name: `slot_items`: each item appears in exactly one slot. The slots d * 64 + p * 2 + j, for j below 2, hold items p * 256 to (p + 1) * 256 - 1, those whose encoder rows lie on pool index p.
All inputs are finite; a program needn't handle non-finite values. No bound on the sum of `token_mask` on one device may be relied on, other than what follows from the above.
Results may differ from the reference program's by a relative error of at most 0.00057.
Values may be sent and summed in bfloat16 or wider, within the bound.
A program may use at most 64 MiB of HBM per device.

```python
import jax
import jax.numpy as jnp
from jax import lax

H = 128
TOK = 32
ITEM_DEV = 64
ITEMS = 8192
PER = 2
GROUP = 256
N_ENC = 4
N_POOL = 32


def draw_slot_items(key, part):
    groups = ITEMS // GROUP
    owners = ITEMS // ITEM_DEV
    keys = jax.random.split(key, groups)
    orders = jax.vmap(lambda single: jax.random.permutation(single, GROUP))(keys).astype(jnp.int32)
    offsets = jnp.arange(groups, dtype=jnp.int32)[:, None] * GROUP
    placed = (orders + offsets).reshape(groups, owners, PER)
    return jnp.transpose(placed, (1, 0, 2)).reshape(ITEMS).astype(jnp.int32)


def plant(values, own_key, smallest, largest):
    longest = values.shape.index(max(values.shape))
    spots = []
    for shift in (0, 1):
        where = [jax.random.randint(jax.random.fold_in(own_key, axis), (), 0, length) for axis, length in enumerate(values.shape)]
        where[longest] = (where[longest] + shift) % values.shape[longest]
        spots.append(tuple(where))
    return values.at[spots[0]].set(smallest).at[spots[1]].set(largest)


def block_levels(key, shape, shards, smallest, largest):
    def one(dim, blocks):
        draws = jax.random.uniform(jax.random.fold_in(jax.random.fold_in(key, 6), dim), (blocks,), jnp.float32, smallest / len(shards), largest / len(shards))
        return jnp.repeat(jnp.exp(draws), shape[dim] // blocks).reshape((-1,) + (1,) * (len(shape) - dim - 1))

    factor_of = one(*shards[0])
    for cut in shards[1:]:
        factor_of = factor_of * one(*cut)
    return factor_of


def gaussian(key, dims, scale, most, cuts=(), kind=jnp.bfloat16):
    gain = block_levels(key, dims, cuts, -0.22, 0.18) if cuts else 1.0
    array = jax.random.normal(key, dims, jnp.float32) * scale * gain
    return jnp.minimum(jnp.maximum(array, -most), most).astype(kind)


def setup_inputs(seed: int = 0) -> dict:
    streams_of = jax.random.split(jax.random.key(seed), 5)
    return {
        "encoded": gaussian(streams_of[0], (ITEMS, TOK, H), 1.0, 6.0, ((0, 32), (1, 4))),
        "slot_items": draw_slot_items(jax.random.fold_in(streams_of[4], 71), 0),
        "lengths": plant(jax.random.randint(streams_of[2], (ITEMS,), 1, TOK + 1), jax.random.fold_in(streams_of[2], 1), 1, TOK).astype(jnp.int32),
        "token_mask": plant((jax.random.randint(streams_of[3], (ITEMS, TOK), 0, 4) < 3).astype(jnp.int32), jax.random.fold_in(streams_of[3], 1), 0, 1),
    }


def chamfer(query, query_valid, other, other_valid):
    dots = jnp.dot(query, other.T, preferred_element_type=jnp.float32)
    dots = dots.reshape(ITEM_DEV, TOK, ITEM_DEV, TOK)
    fore = lax.optimization_barrier(jnp.max(jnp.where(other_valid[None, None] > 0, dots, -4.0), axis=3))
    fore = lax.optimization_barrier(jnp.sum(jnp.where(query_valid[:, :, None] > 0, fore, 0.0), axis=1))
    back = lax.optimization_barrier(jnp.max(jnp.where(query_valid[:, :, None, None] > 0, dots, -4.0), axis=1))
    back = lax.optimization_barrier(jnp.sum(jnp.where(other_valid[None] > 0, back, 0.0), axis=2))
    return 0.5 * (fore + back)

def reference(encoded, slot_items, lengths, token_mask):
    slotted = encoded[slot_items]
    values = slotted.astype(jnp.float32)
    normed = (values / jnp.sqrt(lax.optimization_barrier(jnp.sum(values * values, axis=-1, keepdims=True)) + 1e-06)).astype(jnp.bfloat16)
    position = jnp.arange(TOK, dtype=jnp.int32)[None, :]
    valid = ((position < lengths[:, None]) & ((position == 0) | (token_mask == 1))).astype(jnp.int32)
    owners = N_ENC * N_POOL
    blocks = normed.reshape(owners, ITEM_DEV * TOK, H)
    valid_blocks = valid.reshape(owners, ITEM_DEV, TOK)

    def one_owner(owner):
        tiles = []
        for bit in range(3):
            mate = jnp.bitwise_xor(owner, jnp.int32(1 << bit))
            tiles.append(chamfer(blocks[owner], valid_blocks[owner], blocks[mate], valid_blocks[mate]))
        return jnp.concatenate(tiles, axis=1)
    scores = lax.map(one_owner, jnp.arange(owners, dtype=jnp.int32))
    return scores.reshape(ITEMS, 3 * ITEM_DEV)
```

```python
import functools

import jax
import jax.numpy as jnp
from jax import lax
from jax.experimental import pallas as pl
from jax.experimental.pallas import tpu as pltpu
from jax.sharding import PartitionSpec as P

MESH = pl.DeviceIdType.MESH
NT = (((1,), (1,)), ((), ()))
F32 = jnp.float32
BF16 = jnp.bfloat16


def next_x(x):
    return (2 * x + 1) % 5


def prev_x(x):
    return (3 * x + 2) % 5


def spread(valid, wide):
    for t in range(32):
        wide[t] = jnp.broadcast_to(valid[:, t : t + 1], (64, 128))


def assemble(tiles, wide, out, move, first):
    for a in range(4):
        base = tiles[a * 8 : a * 8 + 8].reshape(128, 128)
        for e in range(4):
            rows = tiles[e * 32 + a * 8 : e * 32 + a * 8 + 8].reshape(128, 128)
            keep = wide[e * 8 : e * 8 + 8, a * 16 : a * 16 + 16, :].reshape(128, 128)
            take = jnp.concatenate([keep * move, (1.0 - keep) * first], axis=1).astype(BF16)
            both = jnp.concatenate([rows, base], axis=0)
            made = jnp.dot(take, both, preferred_element_type=F32).astype(BF16)
            out[e * 8 : e * 8 + 8, a * 16 : a * 16 + 16, :] = made.reshape(8, 16, 128)


def fore_sum(fore, wide, a):
    best = jnp.maximum(fore, pltpu.roll(fore, 64, 1)).reshape(32, 16, 128)
    return jnp.sum(best * wide[:, a * 16 : a * 16 + 16, :], axis=0)


def forward_only(block, other, wide, out):
    for a in range(4):
        left = block[:, a * 16 : a * 16 + 16, :].reshape(512, 128)
        fore = None
        for n in range(8):
            right = other[n * 4 : n * 4 + 4].reshape(256, 128)
            dots = lax.dot_general(left, right, NT, preferred_element_type=F32)
            part = jnp.maximum(dots[:, :128], dots[:, 128:])
            fore = part if fore is None else jnp.maximum(fore, part)
        out[a * 16 : a * 16 + 16, :] = fore_sum(fore, wide, a)


def both_ways(block, other, wide, weight, out):
    for a in range(4):
        left = block[:, a * 16 : a * 16 + 16, :].reshape(512, 128)
        fore = None
        back = None
        for n in range(8):
            right = other[n * 4 : n * 4 + 4].reshape(256, 128)
            dots = lax.dot_general(left, right, NT, preferred_element_type=F32)
            part = jnp.maximum(dots[:, :128], dots[:, 128:])
            fore = part if fore is None else jnp.maximum(fore, part)
            most = jnp.max(dots.reshape(32, 16, 256), axis=0)
            part = most[:, :128] * weight[2 * n : 2 * n + 1, :] + most[:, 128:] * weight[2 * n + 1 : 2 * n + 2, :]
            back = part if back is None else back + part
        back = back + pltpu.roll(back, 64, 1)
        out[a * 16 : a * 16 + 16, :] = 0.5 * (fore_sum(fore, wide, a) + back)


def kernel(
    x_hbm, slots_hbm, lengths_ref, mask_ref, out_ref,
    x, slots, send, tiles_own, tiles_next, block, block_next, block_core,
    valid_own, valid_next, turned, wide, wide_next,
    fore_own, fore_core, score, score_t, score_in,
    load_sem, send_own, send_next, recv_own, recv_next, sem_valid, sem_block, sem_fore, sem_score,
):
    e = lax.axis_index("enc")
    p = lax.axis_index("pool")
    z = p // 8
    xx = (p // 2) % 4
    core = p % 2
    me = e * 32 + p
    nxt = z * 8 + next_x(xx) * 2 + core
    prv = z * 8 + prev_x(xx) * 2 + core
    mate = z * 8 + xx * 2 + (1 - core)

    load_x = pltpu.make_async_copy(x_hbm, x, load_sem.at[0])
    load_slots = pltpu.make_async_copy(slots_hbm, slots, load_sem.at[1])
    load_x.start()
    load_slots.start()

    def peer(i):
        dx = (i // 2) % 4
        dz = (i // 8) % 4
        dy = i // 32
        te = (e + dy) % 4
        tz = (z + dz) % 4
        tx = (xx + dx) % 4
        tc = (core + i) % 2
        return te, tz, tx, tc

    barrier = pltpu.get_barrier_semaphore()

    def greet(i, carry):
        te, tz, tx, tc = peer(128 - i)
        pl.semaphore_signal(barrier, inc=1, device_id=(te, tz * 8 + tx * 2 + tc), device_id_type=MESH)
        return carry

    lax.fori_loop(1, 128, greet, 0)

    length = lengths_ref[...]
    row = lax.broadcasted_iota(jnp.int32, (64, 64), 0)
    col = lax.broadcasted_iota(jnp.int32, (64, 64), 1)
    length_col = jnp.sum(jnp.where(row == col, jnp.broadcast_to(length, (64, 64)), 0), axis=1, keepdims=True)
    position = lax.broadcasted_iota(jnp.int32, (64, 32), 1)
    kept = (position < length_col) & ((position == 0) | (mask_ref[...] == 1))
    valid = jnp.where(kept, 1.0, 0.0).astype(F32)
    valid_own[...] = jnp.concatenate([valid, jnp.zeros((64, 96), F32)], axis=1)
    spread(valid, wide)

    load_x.wait()
    load_slots.wait()

    def gather(d, carry):
        at = d * 64 + p * 2
        first = lax.rem(slots[at], 256)
        second = lax.rem(slots[at + 1], 256)
        both = jnp.concatenate([x[first].astype(F32), x[second].astype(F32)], axis=0)
        scale = lax.rsqrt(jnp.sum(both * both, axis=1, keepdims=True) + 1e-06)
        send[d] = (both * scale).astype(BF16)
        return carry

    lax.fori_loop(0, 128, gather, 0, unroll=8)

    pl.semaphore_wait(barrier, 127)

    def push_own(i, carry):
        te, tz, tx, tc = peer(128 - i)
        tp = tz * 8 + tx * 2 + tc
        pltpu.make_async_remote_copy(
            send.at[te * 32 + tp], tiles_own.at[me], send_own, recv_own, device_id=(te, tp), device_id_type=MESH
        ).start()
        return carry

    def push_next(i, carry):
        te, tz, tx, tc = peer(128 - i)
        tp = tz * 8 + tx * 2 + tc
        unit = te * 32 + tz * 8 + next_x(tx) * 2 + tc
        pltpu.make_async_remote_copy(
            send.at[unit], tiles_next.at[me], send_next, recv_next, device_id=(te, tp), device_id_type=MESH
        ).start()
        return carry

    send_valid = pltpu.make_async_remote_copy(
        valid_own, valid_next, sem_valid.at[0], sem_valid.at[1], device_id=(e, prv), device_id_type=MESH
    )
    send_valid.start()
    pltpu.make_async_copy(send.at[me], tiles_own.at[me], recv_own).start()
    pltpu.make_async_copy(send.at[e * 32 + nxt], tiles_next.at[me], recv_next).start()
    lax.fori_loop(1, 128, push_own, 0)
    lax.fori_loop(1, 128, push_next, 0)

    r = lax.broadcasted_iota(jnp.int32, (128, 128), 0)
    c = lax.broadcasted_iota(jnp.int32, (128, 128), 1)
    move = jnp.where(c == (r % 16) * 8 + r // 16, 1.0, 0.0).astype(F32)
    head = jnp.where(c == (r % 16) * 8, 1.0, 0.0).astype(F32)

    send_valid.wait()
    valid_n = valid_next[...]
    spread(valid_n[:, :32], wide_next)
    turned[...] = valid_n.T[:32, :]
    weight = jnp.concatenate([turned[pl.ds(0, 16, 2), :], turned[pl.ds(1, 16, 2), :]], axis=1)

    pltpu.make_async_copy(tiles_own, tiles_own, recv_own).wait()
    assemble(tiles_own, wide, block, move, head)
    send_block = pltpu.make_async_remote_copy(
        block, block_core, sem_block.at[0], sem_block.at[1], device_id=(e, mate), device_id_type=MESH
    )
    send_block.start()
    send_block.wait()
    forward_only(block, block_core, wide, fore_own)
    send_fore = pltpu.make_async_remote_copy(
        fore_own, fore_core, sem_fore.at[0], sem_fore.at[1], device_id=(e, mate), device_id_type=MESH
    )
    send_fore.start()

    pltpu.make_async_copy(tiles_next, tiles_next, recv_next).wait()
    assemble(tiles_next, wide_next, block_next, move, head)
    both_ways(block, block_next, wide, weight, score)
    score_t[...] = score[...].T[:64, :]
    send_score = pltpu.make_async_remote_copy(
        score_t, score_in, sem_score.at[0], sem_score.at[1], device_id=(e, nxt), device_id_type=MESH
    )
    send_score.start()
    send_fore.wait()
    core_score = 0.5 * (fore_own[:, :64] + fore_core[...].T[:64, :])
    send_score.wait()
    mine = score[:, :64]
    theirs = score_in[...]
    near = jnp.logical_or(xx == 0, xx == 3)
    out_ref[:, 0:64] = core_score
    out_ref[:, 64:128] = jnp.where(near, mine, theirs)
    out_ref[:, 128:192] = jnp.where(near, theirs, mine)
    pltpu.make_async_copy(send.at[pl.ds(0, 127)], send.at[pl.ds(0, 127)], send_own).wait()
    pltpu.make_async_copy(send.at[pl.ds(0, 127)], send.at[pl.ds(0, 127)], send_next).wait()


def shards(encoded, slot_items, lengths, token_mask):
    vmem = pl.BlockSpec(memory_space=pltpu.VMEM)
    hbm = pl.BlockSpec(memory_space=pl.ANY)
    tiles = pltpu.VMEM((128, 16, 128), BF16)
    rows = pltpu.VMEM((32, 64, 128), BF16)
    lanes = pltpu.VMEM((32, 64, 128), F32)
    flat = pltpu.VMEM((64, 128), F32)
    dma = pltpu.SemaphoreType.DMA
    return pl.pallas_call(
        kernel,
        out_shape=jax.ShapeDtypeStruct((64, 192), F32),
        in_specs=[hbm, hbm, vmem, vmem],
        out_specs=vmem,
        scratch_shapes=[
            pltpu.VMEM((256, 8, 128), BF16),
            pltpu.SMEM((8192,), jnp.int32),
            tiles, tiles, tiles, rows, rows, rows,
            flat, flat, pltpu.VMEM((32, 64), F32), lanes, lanes,
            flat, flat, flat, pltpu.VMEM((64, 64), F32), pltpu.VMEM((64, 64), F32),
            dma((2,)), dma, dma, dma, dma, dma((2,)), dma((2,)), dma((2,)), dma((2,)),
        ],
        compiler_params=pltpu.CompilerParams(
            collective_id=0, has_side_effects=True, vmem_limit_bytes=48 * 2**20
        ),
        name="chamfer",
    )(encoded, slot_items, lengths.reshape(1, 64), token_mask)


def solution(mesh):
    in_specs = (P("pool", "enc", None), P(), P(("enc", "pool")), P(("enc", "pool"), None))
    out_specs = P(("enc", "pool"), None)
    return jax.shard_map(shards, mesh=mesh, in_specs=in_specs, out_specs=out_specs, check_vma=False)
```

```python
import functools

import jax
import jax.numpy as jnp
from jax import lax
from jax.experimental import pallas as pl
from jax.experimental.pallas import tpu as pltpu
from jax.sharding import PartitionSpec as P

MESH = pl.DeviceIdType.MESH
NT = (((1,), (1,)), ((), ()))
F32 = jnp.float32
BF16 = jnp.bfloat16


HOP = (0, 1, 2, 1)
FAR = sorted(
    [(x, y, z, c) for y in (2, 1, 3, 0) for z in (2, 1, 3, 0) for x in (2, 1, 3, 0) for c in (0, 1)],
    key=lambda d: -(HOP[d[0]] + HOP[d[1]] + HOP[d[2]]) * 2 - d[3],
)[:-1]


def next_x(x):
    return (2 * x + 1) % 5


def prev_x(x):
    return (3 * x + 2) % 5


def spread(turned, wide):
    valid = jnp.concatenate([turned[...], jnp.zeros((32, 64), F32)], axis=1).T
    for t in range(32):
        wide[t] = jnp.broadcast_to(valid[:64, t : t + 1], (64, 128))


def assemble(tiles, wide, out, move, first):
    for a in range(4):
        base = tiles[a * 8 : a * 8 + 8].reshape(128, 128)
        for e in range(4):
            rows = tiles[e * 32 + a * 8 : e * 32 + a * 8 + 8].reshape(128, 128)
            keep = wide[e * 8 : e * 8 + 8, a * 16 : a * 16 + 16, :].reshape(128, 128)
            take = jnp.concatenate([keep * move, (1.0 - keep) * first], axis=1).astype(BF16)
            both = jnp.concatenate([rows, base], axis=0)
            made = jnp.dot(take, both, preferred_element_type=F32).astype(BF16)
            out[e * 8 : e * 8 + 8, a * 16 : a * 16 + 16, :] = made.reshape(8, 16, 128)


def fore_sum(fore, wide, a):
    best = jnp.maximum(fore, pltpu.roll(fore, 64, 1)).reshape(32, 16, 128)
    return jnp.sum(best * wide[:, a * 16 : a * 16 + 16, :], axis=0)


def forward_only(block, other, wide, out):
    for a in range(4):
        left = block[:, a * 16 : a * 16 + 16, :].reshape(512, 128)
        fore = None
        for n in range(8):
            right = other[n * 4 : n * 4 + 4].reshape(256, 128)
            dots = lax.dot_general(left, right, NT, preferred_element_type=F32)
            part = jnp.maximum(dots[:, :128], dots[:, 128:])
            fore = part if fore is None else jnp.maximum(fore, part)
        out[a * 16 : a * 16 + 16, :] = fore_sum(fore, wide, a)


def both_ways(block, other, wide, weight, out):
    for a in range(4):
        left = block[:, a * 16 : a * 16 + 16, :].reshape(512, 128)
        fore = None
        back = None
        for n in range(8):
            right = other[n * 4 : n * 4 + 4].reshape(256, 128)
            dots = lax.dot_general(left, right, NT, preferred_element_type=F32)
            part = jnp.maximum(dots[:, :128], dots[:, 128:])
            fore = part if fore is None else jnp.maximum(fore, part)
            most = jnp.max(dots.reshape(32, 16, 256), axis=0)
            part = most[:, :128] * weight[2 * n : 2 * n + 1, :] + most[:, 128:] * weight[2 * n + 1 : 2 * n + 2, :]
            back = part if back is None else back + part
        back = back + pltpu.roll(back, 64, 1)
        out[a * 16 : a * 16 + 16, :] = 0.5 * (fore_sum(fore, wide, a) + back)


def kernel(
    x_hbm, slots_hbm, lengths_hbm, mask_hbm, out_ref,
    x, slots, lengths, mask, send, tiles_own, tiles_next, block, block_next, block_core,
    valid_own, valid_next, wide, wide_next,
    fore_own, fore_core, score, score_t, score_in,
    load_sem, send_own, send_next, recv_own, recv_next, sem_valid, sem_block, sem_fore, sem_score,
):
    e = lax.axis_index("enc")
    p = lax.axis_index("pool")
    z = p // 8
    xx = (p // 2) % 4
    core = p % 2
    me = e * 32 + p
    nxt = z * 8 + next_x(xx) * 2 + core
    prv = z * 8 + prev_x(xx) * 2 + core
    mate = z * 8 + xx * 2 + (1 - core)

    load_x = pltpu.make_async_copy(x_hbm, x, load_sem.at[0])
    load_slots = pltpu.make_async_copy(slots_hbm, slots, load_sem.at[1])
    load_lengths = pltpu.make_async_copy(lengths_hbm, lengths, load_sem.at[2])
    load_mask = pltpu.make_async_copy(mask_hbm, mask, load_sem.at[3])
    loads = (load_x, load_slots, load_lengths, load_mask)
    for load in loads:
        load.start()

    def peer(i):
        dx, dy, dz, dc = FAR[i - 1]
        return (e + dy) % 4, (z + dz) % 4, (xx + dx) % 4, (core + dc) % 2

    def peer_old(i):
        dx = (i // 2) % 4
        dz = (i // 8) % 4
        dy = i // 32
        te = (e + dy) % 4
        tz = (z + dz) % 4
        tx = (xx + dx) % 4
        tc = (core + i) % 2
        return te, tz, tx, tc

    barrier = pltpu.get_barrier_semaphore()

    def greet(i, carry):
        te, tz, tx, tc = peer(i)
        pl.semaphore_signal(barrier, inc=1, device_id=(te, tz * 8 + tx * 2 + tc), device_id_type=MESH)
        return carry

    for i in range(1, 128):
        greet(i, 0)

    for load in loads:
        load.wait()

    def gather(d, carry):
        at = d * 64 + p * 2
        first = lax.rem(slots[at], 256)
        second = lax.rem(slots[at + 1], 256)
        both = jnp.concatenate([x[first].astype(F32), x[second].astype(F32)], axis=0)
        scale = lax.rsqrt(jnp.sum(both * both, axis=1, keepdims=True) + 1e-06)
        send[d] = (both * scale).astype(BF16)
        return carry

    lax.fori_loop(0, 128, gather, 0, unroll=8)

    position = lax.broadcasted_iota(jnp.int32, (32, 64), 0)
    kept = (position < lengths[...]) & ((position == 0) | (mask[...] == 1))
    valid_own[...] = jnp.where(kept, 1.0, 0.0).astype(F32)

    pl.semaphore_wait(barrier, 127)

    def push_own(i, carry):
        te, tz, tx, tc = peer(i)
        tp = tz * 8 + tx * 2 + tc
        pltpu.make_async_remote_copy(
            send.at[te * 32 + tp], tiles_own.at[me], send_own, recv_own, device_id=(te, tp), device_id_type=MESH
        ).start()
        return carry

    def push_next(i, carry):
        te, tz, tx, tc = peer(i)
        tp = tz * 8 + tx * 2 + tc
        unit = te * 32 + tz * 8 + next_x(tx) * 2 + tc
        pltpu.make_async_remote_copy(
            send.at[unit], tiles_next.at[me], send_next, recv_next, device_id=(te, tp), device_id_type=MESH
        ).start()
        return carry

    send_valid = pltpu.make_async_remote_copy(
        valid_own, valid_next, sem_valid.at[0], sem_valid.at[1], device_id=(e, prv), device_id_type=MESH
    )
    send_valid.start()
    pltpu.make_async_copy(send.at[me], tiles_own.at[me], recv_own).start()
    pltpu.make_async_copy(send.at[e * 32 + nxt], tiles_next.at[me], recv_next).start()
    for i in range(1, 128):
        push_own(i, 0)
    for i in range(1, 128):
        push_next(i, 0)

    spread(valid_own, wide)
    r = lax.broadcasted_iota(jnp.int32, (128, 128), 0)
    c = lax.broadcasted_iota(jnp.int32, (128, 128), 1)
    move = jnp.where(c == (r % 16) * 8 + r // 16, 1.0, 0.0).astype(F32)
    head = jnp.where(c == (r % 16) * 8, 1.0, 0.0).astype(F32)

    send_valid.wait()
    spread(valid_next, wide_next)
    weight = jnp.concatenate([valid_next[pl.ds(0, 16, 2), :], valid_next[pl.ds(1, 16, 2), :]], axis=1)

    pltpu.make_async_copy(tiles_own, tiles_own, recv_own).wait()
    assemble(tiles_own, wide, block, move, head)
    send_block = pltpu.make_async_remote_copy(
        block, block_core, sem_block.at[0], sem_block.at[1], device_id=(e, mate), device_id_type=MESH
    )
    send_block.start()
    send_block.wait()
    forward_only(block, block_core, wide, fore_own)
    send_fore = pltpu.make_async_remote_copy(
        fore_own, fore_core, sem_fore.at[0], sem_fore.at[1], device_id=(e, mate), device_id_type=MESH
    )
    send_fore.start()

    pltpu.make_async_copy(tiles_next, tiles_next, recv_next).wait()
    assemble(tiles_next, wide_next, block_next, move, head)
    both_ways(block, block_next, wide, weight, score)
    score_t[...] = score[...].T[:64, :]
    send_score = pltpu.make_async_remote_copy(
        score_t, score_in, sem_score.at[0], sem_score.at[1], device_id=(e, nxt), device_id_type=MESH
    )
    send_score.start()
    send_fore.wait()
    core_score = 0.5 * (fore_own[:, :64] + fore_core[...].T[:64, :])
    send_score.wait()
    mine = score[:, :64]
    theirs = score_in[...]
    near = jnp.logical_or(xx == 0, xx == 3)
    out_ref[:, 0:64] = core_score
    out_ref[:, 64:128] = jnp.where(near, mine, theirs)
    out_ref[:, 128:192] = jnp.where(near, theirs, mine)
    pltpu.make_async_copy(send.at[pl.ds(0, 127)], send.at[pl.ds(0, 127)], send_own).wait()
    pltpu.make_async_copy(send.at[pl.ds(0, 127)], send.at[pl.ds(0, 127)], send_next).wait()


def shards(encoded, slot_items, lengths, token_mask):
    vmem = pl.BlockSpec(memory_space=pltpu.VMEM)
    hbm = pl.BlockSpec(memory_space=pltpu.HBM)
    tiles = pltpu.VMEM((128, 16, 128), BF16)
    rows = pltpu.VMEM((32, 64, 128), BF16)
    lanes = pltpu.VMEM((32, 64, 128), F32)
    flat = pltpu.VMEM((64, 128), F32)
    dma = pltpu.SemaphoreType.DMA
    return pl.pallas_call(
        kernel,
        out_shape=jax.ShapeDtypeStruct((64, 192), F32),
        in_specs=[hbm] * 4,
        out_specs=vmem,
        scratch_shapes=[
            pltpu.VMEM((256, 8, 128), BF16),
            pltpu.SMEM((8192,), jnp.int32), pltpu.VMEM((1, 64), jnp.int32), pltpu.VMEM((32, 64), jnp.int32),
            tiles, tiles, tiles, rows, rows, rows,
            pltpu.VMEM((32, 64), F32), pltpu.VMEM((32, 64), F32), lanes, lanes,
            flat, flat, flat, pltpu.VMEM((64, 64), F32), pltpu.VMEM((64, 64), F32),
            dma((4,)), dma, dma, dma, dma, dma((2,)), dma((2,)), dma((2,)), dma((2,)),
        ],
        compiler_params=pltpu.CompilerParams(
            collective_id=0, has_side_effects=True, vmem_limit_bytes=61 * 2**20
        ),
        name="chamfer",
    )(encoded, slot_items, lengths.reshape(1, 64), token_mask.T)


def solution(mesh):
    in_specs = (P("pool", "enc", None), P(), P(("enc", "pool")), P(("enc", "pool"), None))
    out_specs = P(("enc", "pool"), None)
    return jax.shard_map(shards, mesh=mesh, in_specs=in_specs, out_specs=out_specs, check_vma=False)
```

```python
import functools

import jax
import jax.numpy as jnp
from jax import lax
from jax.experimental import pallas as pl
from jax.experimental.pallas import tpu as pltpu
from jax.sharding import PartitionSpec as P

MESH = pl.DeviceIdType.MESH
NT = (((1,), (1,)), ((), ()))
F32 = jnp.float32
BF16 = jnp.bfloat16


HOP = (0, 1, 2, 1)
CHUNK = 127
FAR = sorted(
    [(x, y, z, c) for y in (2, 1, 3, 0) for z in (2, 1, 3, 0) for x in (2, 1, 3, 0) for c in (0, 1)],
    key=lambda d: -(HOP[d[0]] + HOP[d[1]] + HOP[d[2]]) * 2 - d[3],
)[:-1]


def next_x(x):
    return (2 * x + 1) % 5


def prev_x(x):
    return (3 * x + 2) % 5


def spread(turned, wide):
    valid = jnp.concatenate([turned[...], jnp.zeros((32, 64), F32)], axis=1).T
    for t in range(32):
        column = jnp.broadcast_to(valid[:64, t : t + 1], (64, 128))
        for at in range(4):
            wide[at, t] = column[at * 16 : at * 16 + 16]


def group_rows(rank):
    return pl.ds(pl.multiple_of(rank * 8, 8), 8)


def assemble(tiles, wide, out, move, head, rank):
    at = rank // 4
    y = rank % 4
    tokens = pl.ds(pl.multiple_of(y * 8, 8), 8)
    rows = tiles[group_rows(rank)].reshape(128, 128)
    base = tiles[group_rows(at * 4)].reshape(128, 128)
    keep = wide[at, tokens].reshape(128, 128)
    take = jnp.concatenate([keep * move, (1.0 - keep) * head], axis=1).astype(BF16)
    both = jnp.concatenate([rows, base], axis=0)
    made = jnp.dot(take, both, preferred_element_type=F32).astype(BF16)
    out[at, tokens] = made.reshape(8, 16, 128)


def columns(block, n):
    return jnp.concatenate([block[at, u] for u in range(4 * n, 4 * n + 4) for at in range(4)], axis=0)


def fore_sum(fore, wide, a):
    best = jnp.maximum(fore, pltpu.roll(fore, 64, 1)).reshape(32, 16, 128)
    return jnp.sum(best * wide[a], axis=0)


def quarter(block, other, wide, weight, rows, cols, out):
    for i in range(2):
        a = 2 * rows + i
        left = block[a].reshape(512, 128)
        fore = None
        back = None
        for n in range(4):
            right = jnp.concatenate(
                [other[2 * cols + h, u] for u in range(8 * n, 8 * n + 8) for h in range(2)], axis=0
            )
            dots = lax.dot_general(left, right, NT, preferred_element_type=F32)
            part = jnp.maximum(dots[:, :128], dots[:, 128:])
            fore = part if fore is None else jnp.maximum(fore, part)
            most = jnp.max(dots.reshape(32, 16, 256), axis=0)
            part = most[:, :128] * weight[2 * n : 2 * n + 1, :] + most[:, 128:] * weight[2 * n + 1 : 2 * n + 2, :]
            back = part if back is None else back + part
        back = back + pltpu.roll(back, 64, 1)
        back = back + pltpu.roll(back, 32, 1)
        fore = jnp.maximum(fore, pltpu.roll(fore, 64, 1))
        fore = jnp.maximum(fore, pltpu.roll(fore, 32, 1)).reshape(32, 16, 128)
        out[i * 16 : i * 16 + 16, :] = 0.5 * (jnp.sum(fore * wide[a], axis=0) + back)


def both_ways(block, other, wide, weight, out):
    for a in range(4):
        left = block[a].reshape(512, 128)
        fore = None
        back = None
        for n in range(8):
            right = columns(other, n)
            dots = lax.dot_general(left, right, NT, preferred_element_type=F32)
            part = jnp.maximum(dots[:, :128], dots[:, 128:])
            fore = part if fore is None else jnp.maximum(fore, part)
            most = jnp.max(dots.reshape(32, 16, 256), axis=0)
            part = most[:, :128] * weight[2 * n : 2 * n + 1, :] + most[:, 128:] * weight[2 * n + 1 : 2 * n + 2, :]
            back = part if back is None else back + part
        back = back + pltpu.roll(back, 64, 1)
        out[a * 16 : a * 16 + 16, :] = 0.5 * (fore_sum(fore, wide, a) + back)


def kernel(
    x_hbm, slots_hbm, lengths_hbm, mask_hbm, out_ref,
    x, slots, lengths, mask, send, tiles_own, tiles_next, block, block_next, block_core,
    valid_own, valid_next, valid_core, wide, wide_next,
    part_own, part_in, score, score_t, score_in,
    load_sem, send_own, send_next, recv_own, recv_next, sem_valid, sem_out, sem_in, sem_fore, sem_score,
):
    e = lax.axis_index("enc")
    p = lax.axis_index("pool")
    z = p // 8
    xx = (p // 2) % 4
    core = p % 2
    me = e * 32 + p
    nxt = z * 8 + next_x(xx) * 2 + core
    prv = z * 8 + prev_x(xx) * 2 + core
    mate = z * 8 + xx * 2 + (1 - core)

    load_x = pltpu.make_async_copy(x_hbm, x, load_sem.at[0])
    load_slots = pltpu.make_async_copy(slots_hbm, slots, load_sem.at[1])
    load_lengths = pltpu.make_async_copy(lengths_hbm, lengths, load_sem.at[2])
    load_mask = pltpu.make_async_copy(mask_hbm, mask, load_sem.at[3])
    loads = (load_x, load_slots, load_lengths, load_mask)
    for load in loads:
        load.start()

    rank = z * 4 + e
    slot = rank * 8 + xx * 2 + core
    def peer(i):
        dx, dy, dz, dc = FAR[i]
        return (e + dy) % 4, (z + dz) % 4, (xx + dx) % 4, (core + dc) % 2

    barrier = pltpu.get_barrier_semaphore()
    for i in range(127):
        te, tz, tx, tc = peer(i)
        pl.semaphore_signal(barrier, inc=1, device_id=(te, tz * 8 + tx * 2 + tc), device_id_type=MESH)

    for load in loads:
        load.wait()

    def gather(d):
        at = d * 64 + p * 2
        first = lax.rem(slots[at], 256)
        second = lax.rem(slots[at + 1], 256)
        both = jnp.concatenate([x[first].astype(F32), x[second].astype(F32)], axis=0)
        scale = lax.rsqrt(jnp.sum(both * both, axis=1, keepdims=True) + 1e-06)
        send[d] = (both * scale).astype(BF16)

    def push(which, part):
        for i in part:
            te, tz, tx, tc = peer(i)
            if which == 0:
                unit = te * 32 + tz * 8 + tx * 2 + tc
                tiles, sent, got = tiles_own, send_own, recv_own
            else:
                unit = te * 32 + tz * 8 + next_x(tx) * 2 + tc
                tiles, sent, got = tiles_next, send_next, recv_next
            pltpu.make_async_remote_copy(
                send.at[unit], tiles.at[slot], sent, got.at[rank], device_id=(te, tz * 8 + tx * 2 + tc), device_id_type=MESH
            ).start()

    def arrived(tiles, got, k):
        rows = tiles.at[group_rows(k)]
        pltpu.make_async_copy(rows, rows, got.at[k]).wait()

    position = lax.broadcasted_iota(jnp.int32, (32, 64), 0)
    kept = (position < lengths[...]) & ((position == 0) | (mask[...] == 1))
    valid_own[...] = jnp.where(kept, 1.0, 0.0).astype(F32)

    def valid_copy(i, to):
        there = (valid_next, valid_core)[i]
        return pltpu.make_async_remote_copy(
            valid_own, there, sem_valid.at[2 * i], sem_valid.at[2 * i + 1], device_id=(e, to), device_id_type=MESH
        )

    send_valid = (valid_copy(0, prv), valid_copy(1, mate))

    for first in range(0, 127, CHUNK):
        part = range(first, min(first + CHUNK, 127))
        for i in part:
            te, tz, tx, tc = peer(i)
            gather(te * 32 + tz * 8 + tx * 2 + tc)
        if first == 0:
            pl.semaphore_wait(barrier, 127)
            for copy in send_valid:
                copy.start()
        push(0, part)
    gather(me)
    pltpu.make_async_copy(send.at[me], tiles_own.at[slot], recv_own.at[rank]).start()
    pltpu.make_async_copy(send.at[e * 32 + nxt], tiles_next.at[slot], recv_next.at[rank]).start()
    push(1, range(127))

    spread(valid_own, wide)
    r = lax.broadcasted_iota(jnp.int32, (128, 128), 0)
    c = lax.broadcasted_iota(jnp.int32, (128, 128), 1)
    move = jnp.where(c == (r % 16) * 8 + r // 16, 1.0, 0.0).astype(F32)
    head = jnp.where(c == (r % 16) * 8, 1.0, 0.0).astype(F32)

    for copy in send_valid:
        copy.wait()
    spread(valid_next, wide_next)
    weight = jnp.concatenate([valid_next[pl.ds(0, 16, 2), :], valid_next[pl.ds(1, 16, 2), :]], axis=1)
    weights_core = [
        jnp.concatenate([valid_core[pl.ds(k, 8, 4), :][:, h * 32 : h * 32 + 32] for k in range(4)], axis=1) for h in range(2)
    ]

    def core_copy(at):
        return pltpu.make_async_remote_copy(
            block.at[at], block_core.at[at], sem_out.at[at], sem_in.at[at],
            device_id=(e, mate), device_id_type=MESH,
        )

    for dz in (2, 1, 3, 0):
        at = (z + dz) % 4
        for y in range(4):
            arrived(tiles_own, recv_own, at * 4 + y)
        for y in range(4):
            assemble(tiles_own, wide, block, move, head, at * 4 + y)
        core_copy(at).start()
    for dz in (2, 1, 3, 0):
        at = (z + dz) % 4
        for y in range(4):
            arrived(tiles_next, recv_next, at * 4 + y)
        for y in range(4):
            assemble(tiles_next, wide_next, block_next, move, head, at * 4 + y)
    both_ways(block, block_next, wide, weight, score)
    score_t[...] = score[...].T[:64, :]
    send_score = pltpu.make_async_remote_copy(
        score_t, score_in, sem_score.at[0], sem_score.at[1], device_id=(e, nxt), device_id_type=MESH
    )
    send_score.start()
    for at in range(4):
        core_copy(at).wait()
    quarter_copies = []
    for j in range(2):
        rows = j * (1 - core) + core
        cols = j * core
        weight_core = jnp.where(cols == 0, weights_core[0], weights_core[1])
        quarter(block, block_core, wide, weight_core, rows, cols, part_own.at[j])
        copy = pltpu.make_async_remote_copy(
            part_own.at[j], part_in.at[j], sem_fore.at[2 * j], sem_fore.at[2 * j + 1],
            device_id=(e, mate), device_id_type=MESH,
        )
        copy.start()
        quarter_copies.append(copy)
    send_score.wait()
    mine = score[:, :64]
    theirs = score_in[...]
    near = jnp.logical_or(xx == 0, xx == 3)
    out_ref[:, 64:128] = jnp.where(near, mine, theirs)
    out_ref[:, 128:192] = jnp.where(near, theirs, mine)
    for copy in quarter_copies:
        copy.wait()
    q0, q1 = (part_own[j][:, :32] for j in range(2))
    r0, r1 = (part_in[j].T[:32, :] for j in range(2))
    out_ref[0:32, 0:32] = jnp.where(core == 0, q0, r0)
    out_ref[0:32, 32:64] = jnp.where(core == 0, r0, r1)
    out_ref[32:64, 0:32] = jnp.where(core == 0, q1, q0)
    out_ref[32:64, 32:64] = jnp.where(core == 0, r1, q1)
    pltpu.make_async_copy(send.at[pl.ds(0, 127)], send.at[pl.ds(0, 127)], send_own).wait()
    pltpu.make_async_copy(send.at[pl.ds(0, 127)], send.at[pl.ds(0, 127)], send_next).wait()


def shards(encoded, slot_items, lengths, token_mask):
    vmem = pl.BlockSpec(memory_space=pltpu.VMEM)
    hbm = pl.BlockSpec(memory_space=pltpu.HBM)
    tiles = pltpu.VMEM((128, 16, 128), BF16)
    rows = pltpu.VMEM((4, 32, 16, 128), BF16)
    lanes = pltpu.VMEM((4, 32, 16, 128), F32)
    flat = pltpu.VMEM((64, 128), F32)
    dma = pltpu.SemaphoreType.DMA
    return pl.pallas_call(
        kernel,
        out_shape=jax.ShapeDtypeStruct((64, 192), F32),
        in_specs=[hbm] * 4,
        out_specs=vmem,
        scratch_shapes=[
            pltpu.VMEM((256, 8, 128), BF16),
            pltpu.SMEM((8192,), jnp.int32), pltpu.VMEM((1, 64), jnp.int32), pltpu.VMEM((32, 64), jnp.int32),
            tiles, tiles, tiles, rows, rows, rows,
            pltpu.VMEM((32, 64), F32), pltpu.VMEM((32, 64), F32), pltpu.VMEM((32, 64), F32), lanes, lanes,
            pltpu.VMEM((2, 32, 128), F32), pltpu.VMEM((2, 32, 128), F32), flat, pltpu.VMEM((64, 64), F32), pltpu.VMEM((64, 64), F32),
            dma((4,)), dma, dma, dma((16,)), dma((16,)), dma((4,)), dma((4,)), dma((4,)),
            dma((4,)), dma((2,)),
        ],
        compiler_params=pltpu.CompilerParams(
            collective_id=0, has_side_effects=True, vmem_limit_bytes=61 * 2**20
        ),
        name="chamfer",
    )(encoded, slot_items, lengths.reshape(1, 64), token_mask.T)


def solution(mesh):
    in_specs = (P("pool", "enc", None), P(), P(("enc", "pool")), P(("enc", "pool"), None))
    out_specs = P(("enc", "pool"), None)
    return jax.shard_map(shards, mesh=mesh, in_specs=in_specs, out_specs=out_specs, check_vma=False)
```

```python
import functools

import jax
import jax.numpy as jnp
from jax import lax
from jax.experimental import pallas as pl
from jax.experimental.pallas import tpu as pltpu
from jax.sharding import PartitionSpec as P

MESH = pl.DeviceIdType.MESH
NT = (((1,), (1,)), ((), ()))
F32 = jnp.float32
BF16 = jnp.bfloat16


HOP = (0, 1, 2, 1)
CHUNK = 127
FAR = sorted(
    [(x, y, z, c) for y in (2, 1, 3, 0) for z in (2, 1, 3, 0) for x in (2, 1, 3, 0) for c in (0, 1)],
    key=lambda d: -(HOP[d[0]] + HOP[d[1]] + HOP[d[2]]) * 2 - d[3],
)[:-1]


def next_x(x):
    return (2 * x + 1) % 5


def prev_x(x):
    return (3 * x + 2) % 5


def spread(turned, wide):
    valid = jnp.concatenate([turned[...], jnp.zeros((32, 64), F32)], axis=1).T
    for t in range(32):
        column = jnp.broadcast_to(valid[:64, t : t + 1], (64, 128))
        for at in range(4):
            wide[at, t] = column[at * 16 : at * 16 + 16]


def group_rows(rank):
    return pl.ds(pl.multiple_of(rank * 8, 8), 8)


def assemble(tiles, wide, out, move, head, rank):
    at = rank // 4
    y = rank % 4
    tokens = pl.ds(pl.multiple_of(y * 8, 8), 8)
    rows = tiles[group_rows(rank)].reshape(128, 128)
    base = tiles[group_rows(at * 4)].reshape(128, 128)
    keep = wide[at, tokens].reshape(128, 128)
    take = jnp.concatenate([keep * move, (1.0 - keep) * head], axis=1).astype(BF16)
    both = jnp.concatenate([rows, base], axis=0)
    made = jnp.dot(take, both, preferred_element_type=F32).astype(BF16)
    out[at, tokens] = made.reshape(8, 16, 128)


def columns(block, n):
    return jnp.concatenate([block[at, u] for u in range(4 * n, 4 * n + 4) for at in range(4)], axis=0)


def fore_sum(fore, wide, a):
    best = jnp.maximum(fore, pltpu.roll(fore, 64, 1)).reshape(32, 16, 128)
    return jnp.sum(best * wide[a], axis=0)


def both_ways(block, other, wide, weight, out):
    for a in range(4):
        left = block[a].reshape(512, 128)
        fore = None
        back = None
        for n in range(8):
            right = columns(other, n)
            dots = lax.dot_general(left, right, NT, preferred_element_type=F32)
            part = jnp.maximum(dots[:, :128], dots[:, 128:])
            fore = part if fore is None else jnp.maximum(fore, part)
            most = jnp.max(dots.reshape(32, 16, 256), axis=0)
            part = most[:, :128] * weight[2 * n : 2 * n + 1, :] + most[:, 128:] * weight[2 * n + 1 : 2 * n + 2, :]
            back = part if back is None else back + part
        back = back + pltpu.roll(back, 64, 1)
        out[a * 16 : a * 16 + 16, :] = 0.5 * (fore_sum(fore, wide, a) + back)


def kernel(
    x_hbm, slots_hbm, lengths_hbm, mask_hbm, out_ref,
    x, slots, lengths, mask, send, tiles_own, tiles_next, block, block_next, block_core,
    valid_own, valid_next, valid_core, wide, wide_next,
    score_core, score, score_t, score_in,
    load_sem, send_own, send_next, recv_own, recv_next, sem_valid, sem_out, sem_in, sem_score,
):
    e = lax.axis_index("enc")
    p = lax.axis_index("pool")
    z = p // 8
    xx = (p // 2) % 4
    core = p % 2
    me = e * 32 + p
    nxt = z * 8 + next_x(xx) * 2 + core
    prv = z * 8 + prev_x(xx) * 2 + core
    mate = z * 8 + xx * 2 + (1 - core)

    load_x = pltpu.make_async_copy(x_hbm, x, load_sem.at[0])
    load_slots = pltpu.make_async_copy(slots_hbm, slots, load_sem.at[1])
    load_lengths = pltpu.make_async_copy(lengths_hbm, lengths, load_sem.at[2])
    load_mask = pltpu.make_async_copy(mask_hbm, mask, load_sem.at[3])
    loads = (load_x, load_slots, load_lengths, load_mask)
    for load in loads:
        load.start()

    rank = z * 4 + e
    slot = rank * 8 + xx * 2 + core
    def peer(i):
        dx, dy, dz, dc = FAR[i]
        return (e + dy) % 4, (z + dz) % 4, (xx + dx) % 4, (core + dc) % 2

    barrier = pltpu.get_barrier_semaphore()
    for i in range(127):
        te, tz, tx, tc = peer(i)
        pl.semaphore_signal(barrier, inc=1, device_id=(te, tz * 8 + tx * 2 + tc), device_id_type=MESH)

    for load in loads:
        load.wait()

    def gather(d):
        at = d * 64 + p * 2
        first = lax.rem(slots[at], 256)
        second = lax.rem(slots[at + 1], 256)
        both = jnp.concatenate([x[first].astype(F32), x[second].astype(F32)], axis=0)
        scale = lax.rsqrt(jnp.sum(both * both, axis=1, keepdims=True) + 1e-06)
        send[d] = (both * scale).astype(BF16)

    def push(which, part):
        for i in part:
            te, tz, tx, tc = peer(i)
            if which == 0:
                unit = te * 32 + tz * 8 + tx * 2 + tc
                tiles, sent, got = tiles_own, send_own, recv_own
            else:
                unit = te * 32 + tz * 8 + next_x(tx) * 2 + tc
                tiles, sent, got = tiles_next, send_next, recv_next
            pltpu.make_async_remote_copy(
                send.at[unit], tiles.at[slot], sent, got.at[rank], device_id=(te, tz * 8 + tx * 2 + tc), device_id_type=MESH
            ).start()

    def arrived(tiles, got, k):
        rows = tiles.at[group_rows(k)]
        pltpu.make_async_copy(rows, rows, got.at[k]).wait()

    position = lax.broadcasted_iota(jnp.int32, (32, 64), 0)
    kept = (position < lengths[...]) & ((position == 0) | (mask[...] == 1))
    valid_own[...] = jnp.where(kept, 1.0, 0.0).astype(F32)

    def valid_copy(i, to):
        there = (valid_next, valid_core)[i]
        return pltpu.make_async_remote_copy(
            valid_own, there, sem_valid.at[2 * i], sem_valid.at[2 * i + 1], device_id=(e, to), device_id_type=MESH
        )

    send_valid = (valid_copy(0, prv), valid_copy(1, mate))

    for first in range(0, 127, CHUNK):
        part = range(first, min(first + CHUNK, 127))
        for i in part:
            te, tz, tx, tc = peer(i)
            gather(te * 32 + tz * 8 + tx * 2 + tc)
        if first == 0:
            pl.semaphore_wait(barrier, 127)
            for copy in send_valid:
                copy.start()
        push(0, part)
    gather(me)
    pltpu.make_async_copy(send.at[me], tiles_own.at[slot], recv_own.at[rank]).start()
    pltpu.make_async_copy(send.at[e * 32 + nxt], tiles_next.at[slot], recv_next.at[rank]).start()
    push(1, range(127))

    spread(valid_own, wide)
    r = lax.broadcasted_iota(jnp.int32, (128, 128), 0)
    c = lax.broadcasted_iota(jnp.int32, (128, 128), 1)
    move = jnp.where(c == (r % 16) * 8 + r // 16, 1.0, 0.0).astype(F32)
    head = jnp.where(c == (r % 16) * 8, 1.0, 0.0).astype(F32)

    for copy in send_valid:
        copy.wait()
    spread(valid_next, wide_next)
    weight = jnp.concatenate([valid_next[pl.ds(0, 16, 2), :], valid_next[pl.ds(1, 16, 2), :]], axis=1)
    weight_core = jnp.concatenate([valid_core[pl.ds(0, 16, 2), :], valid_core[pl.ds(1, 16, 2), :]], axis=1)

    def core_copy(at):
        return pltpu.make_async_remote_copy(
            block.at[at], block_core.at[at], sem_out.at[at], sem_in.at[at],
            device_id=(e, mate), device_id_type=MESH,
        )

    for dz in (2, 1, 3, 0):
        at = (z + dz) % 4
        for y in range(4):
            arrived(tiles_own, recv_own, at * 4 + y)
        for y in range(4):
            assemble(tiles_own, wide, block, move, head, at * 4 + y)
        core_copy(at).start()
    for dz in (2, 1, 3, 0):
        at = (z + dz) % 4
        for y in range(4):
            arrived(tiles_next, recv_next, at * 4 + y)
        for y in range(4):
            assemble(tiles_next, wide_next, block_next, move, head, at * 4 + y)
    both_ways(block, block_next, wide, weight, score)
    score_t[...] = score[...].T[:64, :]
    send_score = pltpu.make_async_remote_copy(
        score_t, score_in, sem_score.at[0], sem_score.at[1], device_id=(e, nxt), device_id_type=MESH
    )
    send_score.start()
    for at in range(4):
        core_copy(at).wait()
    both_ways(block, block_core, wide, weight_core, score_core)
    out_ref[:, 0:64] = score_core[:, :64]
    send_score.wait()
    mine = score[:, :64]
    theirs = score_in[...]
    near = jnp.logical_or(xx == 0, xx == 3)
    out_ref[:, 64:128] = jnp.where(near, mine, theirs)
    out_ref[:, 128:192] = jnp.where(near, theirs, mine)
    pltpu.make_async_copy(send.at[pl.ds(0, 127)], send.at[pl.ds(0, 127)], send_own).wait()
    pltpu.make_async_copy(send.at[pl.ds(0, 127)], send.at[pl.ds(0, 127)], send_next).wait()


def shards(encoded, slot_items, lengths, token_mask):
    vmem = pl.BlockSpec(memory_space=pltpu.VMEM)
    hbm = pl.BlockSpec(memory_space=pltpu.HBM)
    tiles = pltpu.VMEM((128, 16, 128), BF16)
    rows = pltpu.VMEM((4, 32, 16, 128), BF16)
    lanes = pltpu.VMEM((4, 32, 16, 128), F32)
    flat = pltpu.VMEM((64, 128), F32)
    dma = pltpu.SemaphoreType.DMA
    return pl.pallas_call(
        kernel,
        out_shape=jax.ShapeDtypeStruct((64, 192), F32),
        in_specs=[hbm] * 4,
        out_specs=vmem,
        scratch_shapes=[
            pltpu.VMEM((256, 8, 128), BF16),
            pltpu.SMEM((8192,), jnp.int32), pltpu.VMEM((1, 64), jnp.int32), pltpu.VMEM((32, 64), jnp.int32),
            tiles, tiles, tiles, rows, rows, rows,
            pltpu.VMEM((32, 64), F32), pltpu.VMEM((32, 64), F32), pltpu.VMEM((32, 64), F32), lanes, lanes,
            flat, flat, pltpu.VMEM((64, 64), F32), pltpu.VMEM((64, 64), F32),
            dma((4,)), dma, dma, dma((16,)), dma((16,)), dma((4,)), dma((4,)), dma((4,)),
            dma((2,)),
        ],
        compiler_params=pltpu.CompilerParams(
            collective_id=0, has_side_effects=True, vmem_limit_bytes=61 * 2**20
        ),
        name="chamfer",
    )(encoded, slot_items, lengths.reshape(1, 64), token_mask.T)


def solution(mesh):
    in_specs = (P("pool", "enc", None), P(), P(("enc", "pool")), P(("enc", "pool"), None))
    out_specs = P(("enc", "pool"), None)
    return jax.shard_map(shards, mesh=mesh, in_specs=in_specs, out_specs=out_specs, check_vma=False)
```
